32 devices in a mesh: grp: 2 (over y), chan: 4 (over z), tm: 2 (over x), lag: 2 (over core).
Axes of the slice: x: 2, y: 2, z: 4, core: 2. Of those that a mesh axis runs over, the one named last changes fastest.
Arguments:
- records: bfloat16 [4, 4, 2048, 256], P(('grp', 'tm'), 'chan'), parts along dimension 0, may hold values from -180 to 180, as said below
- dead_mask: int32 [512], P('grp'), parts along dimension 0, may hold values 0 or 1
- block_map: int32 [8], P('grp'), parts along dimension 0, may hold values from 0 to 3, each once
Outputs:
- correlations: float32 [4096, 2, 256], P(('grp', 'tm', 'lag'), None, 'chan'), parts along dimension 0
The draws below stay inside these ranges and needn't reach their ends.
There are 2 independent parts, one for each index of `grp`. The reference program is written for one: setup_inputs(seed, part) draws one part's arguments, and reference() takes and returns one part's arrays. A program takes and returns all parts, laid end to end along the dimension named above; each array names one. Nothing has to cross between parts.
Inputs may be any that keep to these rules, and one draw needn't show every extreme that they name: block_map is a permutation of the block numbers. `records`: values are finite.
All inputs are finite; a program needn't handle non-finite values.
Results may differ from the reference program's by a relative error of at most 0.015.
Values may be sent and summed in bfloat16 or wider, within the bound.
A program may use at most 64 MiB of HBM per device.

```python
import math
import jax
import jax.numpy as jnp
from jax import lax

SAMPLES = 2048
CH_DEV = 64
BAND = 16
CHAN_BLOCKS = 4
CH = 256
FRAMES = 4
GROUPS = 2
HALF = 1024
LAGS = 2048
ROUNDS = 2


def draw_records(key, part):
    base_key = jax.random.fold_in(key, 11)
    chan_key = jax.random.fold_in(key, 12)
    frame_key = jax.random.fold_in(key, 13)
    noise = jnp.clip(jax.random.normal(base_key, (GROUPS, FRAMES, SAMPLES, CH), jnp.float32), -6.0, 6.0)
    chan_gain = jnp.exp(jax.random.uniform(chan_key, (CH,), jnp.float32, math.log(0.3), math.log(3.0)))
    frame_gain = jnp.exp(jax.random.uniform(frame_key, (GROUPS, FRAMES, 1, 1), jnp.float32, 0.0, math.log(10.0)))
    return (noise * chan_gain[None, None, None, :] * frame_gain).astype(jnp.bfloat16)


def place_ends(result, own_key, smallest, top_value):
    spot = [jax.random.randint(jax.random.fold_in(own_key, axis), (), 0, length) for axis, length in enumerate(result.shape)]
    longest = result.shape.index(max(result.shape))
    neighbour = spot[:longest] + [(spot[longest] + 1) % result.shape[longest]] + spot[longest + 1:]
    return result.at[tuple(spot)].set(smallest).at[tuple(neighbour)].set(top_value)


def setup_inputs(seed: int = 0, part: int = 0) -> dict:
    streams_of = jax.random.split(jax.random.key(seed), 4)
    part_splits = jax.random.split(jax.random.fold_in(streams_of[3], part), 4)
    return {
        "records": draw_records(jax.random.fold_in(jax.random.fold_in(streams_of[3], part), 71), part),
        "dead_mask": place_ends((jax.random.randint(part_splits[1], (CH,), 0, 10) < 9).astype(jnp.int32), jax.random.fold_in(part_splits[1], 1), 0, 1),
        "block_map": jax.random.permutation(part_splits[2], CHAN_BLOCKS).astype(jnp.int32),
    }


def trig_table(row_index, bin_index, samples):
    phase = row_index[:, None] * bin_index[None, :] % samples
    angle = phase.astype(jnp.float32) * (2.0 * math.pi / samples)
    return jnp.concatenate([jnp.cos(angle), -jnp.sin(angle)], axis=1).astype(jnp.bfloat16)

def band_gain(bin_index, samples):
    freq = bin_index.astype(jnp.float32)
    ramp_width = float(max(samples // 128, 1))
    lower = jnp.clip((freq - float(samples // 256)) / ramp_width, 0.0, 1.0)
    upper = jnp.clip((0.45 * samples - freq) / ramp_width, 0.0, 1.0)
    return lower * upper

def whiten(spectra, bin_index, samples, band_size):
    values = spectra.astype(jnp.float32)
    half_bins = values.shape[-1] // 2
    real_part = values[..., :half_bins]
    imag_part = values[..., half_bins:]
    power = real_part * real_part + imag_part * imag_part
    frame_total = power.shape[0]
    chan_total = power.shape[1]
    banded = lax.optimization_barrier(jnp.mean(power.reshape(frame_total, chan_total, half_bins // band_size, band_size), axis=(0, 3)))
    factor = jnp.repeat(1.0 / jnp.sqrt(banded + 1e-06), band_size, axis=1) * band_gain(bin_index, samples)[None, :]
    factor = jnp.concatenate([factor, factor], axis=1)
    return (values * factor[None]).astype(jnp.bfloat16)

def cross_spectrum(own, other):
    half_bins = own.shape[-1] // 2
    own_real = own[..., :half_bins].astype(jnp.float32)
    own_imag = own[..., half_bins:].astype(jnp.float32)
    other_real = other[..., :half_bins].astype(jnp.float32)
    other_imag = other[..., half_bins:].astype(jnp.float32)
    real_sum = lax.optimization_barrier(jnp.sum(own_real * other_real + own_imag * other_imag, axis=0))
    imag_sum = lax.optimization_barrier(jnp.sum(own_imag * other_real - own_real * other_imag, axis=0))
    return jnp.concatenate([real_sum, imag_sum], axis=1)

def reference(records, dead_mask, block_map):
    live = records * dead_mask.astype(jnp.bfloat16)[None, None, None, :]
    ordered = jnp.take(live.reshape(GROUPS, FRAMES, SAMPLES, CHAN_BLOCKS, CH_DEV), block_map, axis=3)
    ordered = ordered.reshape(GROUPS, FRAMES, SAMPLES, CH)
    bin_index = jnp.arange(HALF, dtype=jnp.int32)
    row_index = jnp.arange(SAMPLES, dtype=jnp.int32)
    forward = trig_table(row_index, bin_index, SAMPLES).astype(jnp.float32)
    inverse = trig_table(row_index + HALF, bin_index, SAMPLES).astype(jnp.float32)
    stacked_total = jnp.zeros((SAMPLES, ROUNDS * CH), jnp.float32)
    for group in range(GROUPS):
        frames_now = jnp.transpose(ordered[group], (0, 2, 1)).reshape(FRAMES * CH, SAMPLES)
        spectra = jnp.dot(frames_now.astype(jnp.float32), forward, preferred_element_type=jnp.float32)
        spectra = spectra.reshape(FRAMES, CH, 2 * HALF).astype(jnp.bfloat16)
        whitened = whiten(spectra, bin_index, SAMPLES, BAND)
        columns = []
        for offset in range(ROUNDS):
            partner = jnp.roll(whitened, (offset + 1) * CH_DEV, axis=1)
            columns.append(cross_spectrum(whitened, partner))
        flat = jnp.stack(columns).astype(jnp.bfloat16).reshape(ROUNDS * CH, 2 * HALF)
        stacked_total = stacked_total + lax.dot_general(inverse, flat.astype(jnp.float32), (((1,), (1,)), ((), ())), preferred_element_type=jnp.float32)
    norm = 1.0 / math.sqrt(HALF * FRAMES * GROUPS)
    return (stacked_total * norm).reshape(LAGS, ROUNDS, CH)
```

```python
import functools
import math

import jax
import jax.numpy as jnp
import ml_dtypes
import numpy as np
from jax import lax
from jax.experimental import pallas as pl
from jax.experimental.pallas import tpu as pltpu
from jax.sharding import PartitionSpec as P

BAND = 16
MESH = pl.DeviceIdType.MESH


def trig_tables(samples, chans, times, lags):
    half = samples // 2
    bins = half // (lags * chans)
    rows = np.arange(samples, dtype=np.int64)
    phase = (rows[:, None] * np.arange(half)[None, :]) % samples
    angle = phase.astype(np.float32) * np.float32(2.0 * math.pi / samples)
    cosine = np.cos(angle).astype(ml_dtypes.bfloat16)
    sine = (-np.sin(angle)).astype(ml_dtypes.bfloat16)
    both = np.stack([a.reshape(samples, lags, chans, bins) for a in (cosine, sine)])
    both = both.transpose(2, 3, 1, 0, 4).reshape(lags, chans, samples, 2 * bins)
    forward = np.ascontiguousarray(both.transpose(0, 1, 3, 2))
    inverse = both[:, :, (rows + half) % samples]
    inverse = inverse.reshape(lags, chans, times, lags, samples // (times * lags), 2 * bins)
    inverse = inverse.transpose(0, 1, 3, 2, 4, 5).reshape(lags, chans, samples, 2 * bins)
    return forward, np.ascontiguousarray(inverse)


def kernel(
    chans, times, lags, rounds, norm,
    map_ref, mask_ref, x_ref, forward_hbm, inverse_hbm, out_ref,
    forward, inverse, pick, ordered, spec_out, spec, cross_out, cross, partial, core_out, core_in,
    time_out, time_in,
    forward_sem, inverse_sem, spec_send, spec_recv, cross_send, cross_recv, core_send, core_recv,
    time_send, time_recv,
):
    me, core, group = lax.axis_index("chan"), lax.axis_index("lag"), lax.axis_index("tm")
    samples, width_all = x_ref.shape
    width = width_all // chans
    bins = forward.shape[1] // 2
    lag_rows = out_ref.shape[0]

    def around(index, by, count):
        return lax.rem(index + by + count, count)

    barrier = pltpu.get_barrier_semaphore()
    for axis, index, count in (("chan", me, chans), ("lag", core, lags), ("tm", group, times)):
        for by in range(1, count):
            pl.semaphore_signal(
                barrier, inc=1, device_id={axis: around(index, by, count)}, device_id_type=MESH
            )

    def load_forward(s):
        return pltpu.make_async_copy(
            forward_hbm.at[core, around(me, s, chans)], forward.at[s], forward_sem.at[s]
        )

    def load_inverse(s):
        return pltpu.make_async_copy(
            inverse_hbm.at[core, around(me, -s, chans)], inverse.at[s], inverse_sem.at[s]
        )

    def send_spec(s):
        return pltpu.make_async_remote_copy(
            src_ref=spec_out.at[s], dst_ref=spec.at[s],
            send_sem=spec_send.at[s], recv_sem=spec_recv.at[s],
            device_id={"chan": around(me, s, chans)}, device_id_type=MESH,
        )

    def send_cross(s):
        return pltpu.make_async_remote_copy(
            src_ref=cross_out.at[around(me, s, chans)], dst_ref=cross.at[s],
            send_sem=cross_send.at[s], recv_sem=cross_recv.at[s],
            device_id={"chan": around(me, s, chans)}, device_id_type=MESH,
        )

    def send_core(s):
        return pltpu.make_async_remote_copy(
            src_ref=core_out.at[s], dst_ref=core_in.at[s],
            send_sem=core_send.at[s], recv_sem=core_recv.at[s],
            device_id={"lag": around(core, s, lags)}, device_id_type=MESH,
        )

    def send_time(s):
        return pltpu.make_async_remote_copy(
            src_ref=time_out.at[s], dst_ref=time_in.at[s],
            send_sem=time_send.at[s], recv_sem=time_recv.at[s],
            device_id={"tm": around(group, s, times)}, device_id_type=MESH,
        )

    def each(low, high, work):
        def step(s, carry):
            work(s)
            return carry

        lax.fori_loop(low, high, step, 0)

    each(1, chans, lambda s: load_forward(s).start())
    load_forward(0).start()
    each(0, chans, lambda s: load_inverse(s).start())

    for p in range(chans):
        source = map_ref[p] * width + lax.broadcasted_iota(jnp.int32, (width, width_all), 0)
        channel = lax.broadcasted_iota(jnp.int32, (width, width_all), 1)
        kept = jnp.where(source == channel, mask_ref[...], 0)
        pick[p * width:(p + 1) * width, :] = kept.astype(jnp.float32).astype(jnp.bfloat16)
    tile = min(512, samples)

    def order(i):
        rows = pl.ds(pl.multiple_of(i * tile, tile), tile)
        ordered[rows, :] = lax.dot_general(
            x_ref[rows, :], pick[...], (((1,), (1,)), ((), ())),
            preferred_element_type=jnp.float32,
        ).astype(jnp.bfloat16)

    each(0, samples // tile, order)

    def transform(s):
        load_forward(s).wait()
        return jnp.dot(
            forward[s], ordered[...], preferred_element_type=jnp.float32
        ).astype(jnp.bfloat16)

    pl.semaphore_wait(barrier, chans + lags + times - 3)

    def transform_and_send(s):
        spec_out[s] = transform(s)
        send_spec(s).start()

    each(1, chans, transform_and_send)
    spec[0] = transform(0)
    each(1, chans, lambda s: send_spec(s).wait_recv())

    part = min(32, bins)
    freq_base = core * (bins * chans) + me * bins

    def cross_part(i):
        low = pl.multiple_of(i * part, part)
        re_rows = pl.ds(low, part)
        im_rows = pl.ds(pl.multiple_of(bins + i * part, part), part)
        power = jnp.zeros((part, width_all), jnp.float32)
        for f in range(chans):
            re = spec[f, re_rows, :].astype(jnp.float32)
            im = spec[f, im_rows, :].astype(jnp.float32)
            power = power + (re * re + im * im)
        banded = jnp.sum(power.reshape(part // BAND, BAND, width_all), axis=1, keepdims=True)
        scale = 1.0 / jnp.sqrt(banded / float(chans * BAND) + 1e-06)
        scale = jnp.broadcast_to(scale, (part // BAND, BAND, width_all)).reshape(part, width_all)
        freq = (freq_base + low + lax.broadcasted_iota(jnp.int32, (part, width_all), 0)).astype(
            jnp.float32
        )
        ramp_width = float(max(samples // 128, 1))
        lower = jnp.clip((freq - float(samples // 256)) / ramp_width, 0.0, 1.0)
        upper = jnp.clip((0.45 * samples - freq) / ramp_width, 0.0, 1.0)
        factor = scale * (lower * upper)
        re_sum = [jnp.zeros((part, width_all), jnp.float32) for _ in range(rounds)]
        im_sum = [jnp.zeros((part, width_all), jnp.float32) for _ in range(rounds)]
        for f in range(chans):
            re = (spec[f, re_rows, :].astype(jnp.float32) * factor).astype(jnp.bfloat16)
            im = (spec[f, im_rows, :].astype(jnp.float32) * factor).astype(jnp.bfloat16)
            re, im = re.astype(jnp.float32), im.astype(jnp.float32)
            for r in range(rounds):
                re_far = pltpu.roll(re, (r + 1) * width, 1)
                im_far = pltpu.roll(im, (r + 1) * width, 1)
                re_sum[r] = re_sum[r] + (re * re_far + im * im_far)
                im_sum[r] = im_sum[r] + (im * re_far - re * im_far)
        for c in range(chans):
            own = slice(c * width, (c + 1) * width)
            cross_out[c, re_rows, :] = jnp.concatenate(
                [a[:, own] for a in re_sum], axis=1
            ).astype(jnp.bfloat16)
            cross_out[c, im_rows, :] = jnp.concatenate(
                [a[:, own] for a in im_sum], axis=1
            ).astype(jnp.bfloat16)

    each(0, bins // part, cross_part)
    each(1, chans, lambda s: send_cross(s).start())
    cross[0] = cross_out[me]

    def invert(s):
        load_inverse(s).wait()
        return jnp.dot(inverse[s], cross[s], preferred_element_type=jnp.float32)

    partial[...] = invert(0)

    def invert_more(s):
        send_cross(s).wait_recv()
        partial[...] += invert(s)

    each(1, chans, invert_more)

    def rows_of(lag_block):
        count = times * lag_rows
        return pl.ds(pl.multiple_of(lag_block * count, count), count)

    for s in range(1, lags):
        core_out[s] = partial[rows_of(around(core, s, lags)), :].astype(jnp.bfloat16)
        send_core(s).start()
    total = partial[rows_of(core), :]
    for s in range(1, lags):
        send_core(s).wait_recv()
        total = total + core_in[s].astype(jnp.float32)
    partial[0:times * lag_rows, :] = total

    def own_lags(index):
        return partial[pl.ds(pl.multiple_of(index * lag_rows, lag_rows), lag_rows), :]

    for s in range(1, times):
        time_out[s] = own_lags(around(group, s, times)).astype(jnp.bfloat16)
        send_time(s).start()
    result = own_lags(group)
    for s in range(1, times):
        send_time(s).wait_recv()
        result = result + time_in[s].astype(jnp.float32)
    out_ref[...] = result * norm

    each(1, chans, lambda s: send_spec(s).wait_send())
    each(1, chans, lambda s: send_cross(s).wait_send())
    for s in range(1, lags):
        send_core(s).wait_send()
    for s in range(1, times):
        send_time(s).wait_send()


def body(forward_table, inverse_table, records, dead_mask, block_map):
    chans, lags, times = lax.axis_size("chan"), lax.axis_size("lag"), lax.axis_size("tm")
    samples, width_all = records.shape[2:]
    width = width_all // chans
    rounds = min(4, chans // 2)
    bins = samples // (2 * lags * chans)
    lag_rows = samples // (times * lags)
    columns = rounds * width
    norm = 1.0 / math.sqrt(samples // 2 * chans * times)
    vmem = pl.BlockSpec(memory_space=pltpu.VMEM)
    bf16, dma = jnp.bfloat16, pltpu.SemaphoreType.DMA
    stacked = pl.pallas_call(
        functools.partial(kernel, chans, times, lags, rounds, norm),
        out_shape=jax.ShapeDtypeStruct((lag_rows, columns), jnp.float32),
        in_specs=[
            pl.BlockSpec(memory_space=pltpu.SMEM), vmem, vmem,
            pl.BlockSpec(memory_space=pl.ANY), pl.BlockSpec(memory_space=pl.ANY),
        ],
        out_specs=vmem,
        scratch_shapes=[
            pltpu.VMEM((chans, 2 * bins, samples), bf16),
            pltpu.VMEM((chans, samples, 2 * bins), bf16),
            pltpu.VMEM((width_all, width_all), bf16),
            pltpu.VMEM((samples, width_all), bf16),
            pltpu.VMEM((chans, 2 * bins, width_all), bf16),
            pltpu.VMEM((chans, 2 * bins, width_all), bf16),
            pltpu.VMEM((chans, 2 * bins, columns), bf16),
            pltpu.VMEM((chans, 2 * bins, columns), bf16),
            pltpu.VMEM((samples, columns), jnp.float32),
            pltpu.VMEM((lags, times * lag_rows, columns), bf16),
            pltpu.VMEM((lags, times * lag_rows, columns), bf16),
            pltpu.VMEM((times, lag_rows, columns), bf16),
            pltpu.VMEM((times, lag_rows, columns), bf16),
            dma((chans,)), dma((chans,)), dma((chans,)), dma((chans,)), dma((chans,)), dma((chans,)),
            dma((lags,)), dma((lags,)), dma((times,)), dma((times,)),
        ],
        compiler_params=pltpu.CompilerParams(
            collective_id=0, has_side_effects=True, vmem_limit_bytes=58 * 1024 * 1024
        ),
    )(block_map, dead_mask.reshape(1, width_all), records[0, 0], forward_table, inverse_table)
    return stacked.reshape(lag_rows, rounds, width)


def solution(mesh):
    shape = mesh.shape

    def run(records, dead_mask, block_map):
        tables = trig_tables(records.shape[2], shape["chan"], shape["tm"], shape["lag"])
        forward_table, inverse_table = (jnp.asarray(a) for a in tables)
        return jax.shard_map(
            body,
            mesh=mesh,
            in_specs=(P(), P(), P(("grp", "tm"), "chan", None, None), P("grp"), P("grp")),
            out_specs=P(("grp", "tm", "lag"), None, "chan"),
            check_vma=False,
        )(forward_table, inverse_table, records, dead_mask, block_map)

    return run
```

```python
import functools
import math

import jax
import jax.numpy as jnp
import ml_dtypes
import numpy as np
from jax import lax
from jax.experimental import pallas as pl
from jax.experimental.pallas import tpu as pltpu
from jax.sharding import PartitionSpec as P

BAND = 16
HALVES = 2
MESH = pl.DeviceIdType.MESH


def trig_tables(samples, chans, times, lags, halves):
    half = samples // 2
    bins = half // (lags * chans * halves)
    rows = np.arange(samples, dtype=np.int64)
    phase = (np.arange(half)[:, None] * rows[None, :]) % samples
    angle = phase.astype(np.float32) * np.float32(2.0 * math.pi / samples)
    cosine = np.cos(angle).astype(ml_dtypes.bfloat16)
    sine = (-np.sin(angle)).astype(ml_dtypes.bfloat16)
    both = np.stack([a.reshape(lags, chans, halves, bins, samples) for a in (cosine, sine)], axis=3)
    forward = both.reshape(lags, chans, halves, 2 * bins, samples)
    inverse = both.reshape(lags, chans, 2 * halves * bins, samples)[..., (rows + half) % samples]
    inverse = inverse.reshape(inverse.shape[:3] + (times * lags, samples // (times * lags)))
    return forward, np.ascontiguousarray(inverse.transpose(3, 0, 1, 2, 4))


def kernel(
    chans, times, lags, rounds, halves, norm,
    map_ref, mask_ref, x_ref, forward_hbm, inverse_hbm, out_ref,
    forward, inverse, pick, ordered, spec_out, spec, cross_out, cross, far, summed,
    forward_sem, inverse_sem, spec_send, spec_recv, cross_send, cross_recv, far_send, far_recv,
    core_send, core_recv,
):
    me, core, group = lax.axis_index("chan"), lax.axis_index("lag"), lax.axis_index("tm")
    samples, width_all = x_ref.shape
    width = width_all // chans
    bins = forward.shape[2] // 2
    columns, lag_rows = out_ref.shape

    def around(index, by, count):
        return lax.rem(index + by + count, count)

    barrier = pltpu.get_barrier_semaphore()
    for axis, index, count in (("chan", me, chans), ("lag", core, lags), ("tm", group, times)):
        for by in range(1, count):
            pl.semaphore_signal(
                barrier, inc=1, device_id={axis: around(index, by, count)}, device_id_type=MESH
            )

    def load_forward(s, h):
        return pltpu.make_async_copy(
            forward_hbm.at[core, around(me, s, chans), h], forward.at[s, h], forward_sem.at[s, h]
        )

    def load_inverse(v, s):
        return pltpu.make_async_copy(
            inverse_hbm.at[group * lags + core, around(core, -v, lags), around(me, -s, chans)],
            inverse.at[v, s], inverse_sem.at[v, s],
        )

    def send_spec(s, h):
        return pltpu.make_async_remote_copy(
            src_ref=spec_out.at[s, h], dst_ref=spec.at[s, h],
            send_sem=spec_send.at[s, h], recv_sem=spec_recv.at[s, h],
            device_id={"chan": around(me, s, chans)}, device_id_type=MESH,
        )

    def send_cross(s, h):
        return pltpu.make_async_remote_copy(
            src_ref=cross_out.at[around(me, s, chans), h], dst_ref=cross.at[s, h],
            send_sem=cross_send.at[s, h], recv_sem=cross_recv.at[s, h],
            device_id={"chan": around(me, s, chans)}, device_id_type=MESH,
        )

    def send_far(u, s, h):
        return pltpu.make_async_remote_copy(
            src_ref=cross.at[s, h], dst_ref=far.at[u, s, h],
            send_sem=far_send.at[u, s, h], recv_sem=far_recv.at[u, s, h],
            device_id={"tm": around(group, u, times)}, device_id_type=MESH,
        )

    def send_core(v, s, h):
        return pltpu.make_async_remote_copy(
            src_ref=summed.at[0, s, h], dst_ref=summed.at[v, s, h],
            send_sem=core_send.at[v, s, h], recv_sem=core_recv.at[v, s, h],
            device_id={"lag": around(core, v, lags)}, device_id_type=MESH,
        )

    def each(low, high, work):
        def step(s, carry):
            work(s)
            return carry

        lax.fori_loop(low, high, step, 0)

    for h in range(halves):
        each(1, chans, lambda s: load_forward(s, h).start())
    for h in range(halves):
        load_forward(0, h).start()
    for v in range(lags):
        each(0, chans, lambda s: load_inverse(v, s).start())

    for p in range(chans):
        source = map_ref[p] * width + lax.broadcasted_iota(jnp.int32, (width, width_all), 0)
        channel = lax.broadcasted_iota(jnp.int32, (width, width_all), 1)
        kept = jnp.where(source == channel, mask_ref[...], 0)
        pick[p * width:(p + 1) * width, :] = kept.astype(jnp.float32).astype(jnp.bfloat16)
    tile = min(512, samples)

    def order(i):
        rows = pl.ds(pl.multiple_of(i * tile, tile), tile)
        ordered[rows, :] = lax.dot_general(
            x_ref[rows, :], pick[...], (((1,), (1,)), ((), ())),
            preferred_element_type=jnp.float32,
        ).astype(jnp.bfloat16)

    each(0, samples // tile, order)

    def transform(s, h):
        load_forward(s, h).wait()
        return jnp.dot(
            forward[s, h], ordered[...], preferred_element_type=jnp.float32
        ).astype(jnp.bfloat16)

    pl.semaphore_wait(barrier, chans + lags + times - 3)

    for h in range(halves):
        def transform_and_send(s):
            spec_out[s, h] = transform(s, h)
            send_spec(s, h).start()

        each(1, chans, transform_and_send)
    for h in range(halves):
        spec[0, h] = transform(0, h)

    part = min(32, bins)

    def cross_part(h, i):
        low = pl.multiple_of(i * part, part)
        re_rows = pl.ds(low, part)
        im_rows = pl.ds(pl.multiple_of(bins + i * part, part), part)
        power = jnp.zeros((part, width_all), jnp.float32)
        for f in range(chans):
            re = spec[f, h, re_rows, :].astype(jnp.float32)
            im = spec[f, h, im_rows, :].astype(jnp.float32)
            power = power + (re * re + im * im)
        banded = jnp.sum(power.reshape(part // BAND, BAND, width_all), axis=1, keepdims=True)
        scale = 1.0 / jnp.sqrt(banded / float(chans * BAND) + 1e-06)
        scale = jnp.broadcast_to(scale, (part // BAND, BAND, width_all)).reshape(part, width_all)
        freq_base = ((core * chans + me) * halves + h) * bins + low
        freq = (freq_base + lax.broadcasted_iota(jnp.int32, (part, width_all), 0)).astype(
            jnp.float32
        )
        ramp_width = float(max(samples // 128, 1))
        lower = jnp.clip((freq - float(samples // 256)) / ramp_width, 0.0, 1.0)
        upper = jnp.clip((0.45 * samples - freq) / ramp_width, 0.0, 1.0)
        factor = scale * (lower * upper)
        re_sum = [jnp.zeros((part, width_all), jnp.float32) for _ in range(rounds)]
        im_sum = [jnp.zeros((part, width_all), jnp.float32) for _ in range(rounds)]
        for f in range(chans):
            re = (spec[f, h, re_rows, :].astype(jnp.float32) * factor).astype(jnp.bfloat16)
            im = (spec[f, h, im_rows, :].astype(jnp.float32) * factor).astype(jnp.bfloat16)
            re, im = re.astype(jnp.float32), im.astype(jnp.float32)
            for r in range(rounds):
                re_far = pltpu.roll(re, (r + 1) * width, 1)
                im_far = pltpu.roll(im, (r + 1) * width, 1)
                re_sum[r] = re_sum[r] + (re * re_far + im * im_far)
                im_sum[r] = im_sum[r] + (im * re_far - re * im_far)
        for c in range(chans):
            own = slice(c * width, (c + 1) * width)
            cross_out[c, h, re_rows, :] = jnp.concatenate(
                [a[:, own] for a in re_sum], axis=1
            ).astype(jnp.bfloat16)
            cross_out[c, h, im_rows, :] = jnp.concatenate(
                [a[:, own] for a in im_sum], axis=1
            ).astype(jnp.bfloat16)

    def start_far(s, h):
        for u in range(1, times):
            send_far(u, s, h).start()

    def sum_groups(s, h):
        total = cross[s, h].astype(jnp.float32)
        for u in range(1, times):
            send_far(u, s, h).wait_recv()
            total = total + far[u, s, h].astype(jnp.float32)
        summed[0, s, h] = total.astype(jnp.bfloat16)
        for v in range(1, lags):
            send_core(v, s, h).start()

    def pass_on(s, h):
        send_cross(s, h).wait_recv()
        start_far(s, h)

    for h in range(halves):
        each(1, chans, lambda s: send_spec(s, h).wait_recv())
        each(0, bins // part, lambda i: cross_part(h, i))
        each(1, chans, lambda s: send_cross(s, h).start())
        cross[0, h] = cross_out[me, h]
        start_far(0, h)
    for h in range(halves):
        each(1, chans, lambda s: pass_on(s, h))
        each(0, chans, lambda s: sum_groups(s, h))

    def invert(v):
        each(0, chans, lambda s: load_inverse(v, s).wait())
        depth = chans * halves * 2 * bins
        return lax.dot_general(
            summed[v].reshape(depth, columns), inverse[v].reshape(depth, lag_rows),
            (((0,), (0,)), ((), ())), preferred_element_type=jnp.float32,
        )

    result = invert(0)
    for v in range(1, lags):
        for h in range(halves):
            each(0, chans, lambda s: send_core(v, s, h).wait_recv())
        result = result + invert(v)
    out_ref[...] = result * norm

    for h in range(halves):
        each(1, chans, lambda s: send_spec(s, h).wait_send())
        each(1, chans, lambda s: send_cross(s, h).wait_send())
        for u in range(1, times):
            each(0, chans, lambda s: send_far(u, s, h).wait_send())
        for v in range(1, lags):
            each(0, chans, lambda s: send_core(v, s, h).wait_send())


def body(forward_table, inverse_table, records, dead_mask, block_map):
    chans, lags, times = lax.axis_size("chan"), lax.axis_size("lag"), lax.axis_size("tm")
    samples, width_all = records.shape[2:]
    width = width_all // chans
    rounds = min(4, chans // 2)
    halves = HALVES
    bins = samples // (2 * lags * chans * halves)
    lag_rows = samples // (times * lags)
    columns = rounds * width
    norm = 1.0 / math.sqrt(samples // 2 * chans * times)
    vmem = pl.BlockSpec(memory_space=pltpu.VMEM)
    bf16, dma = jnp.bfloat16, pltpu.SemaphoreType.DMA
    piece = (chans, halves, 2 * bins)
    stacked = pl.pallas_call(
        functools.partial(kernel, chans, times, lags, rounds, halves, norm),
        out_shape=jax.ShapeDtypeStruct((columns, lag_rows), jnp.float32),
        in_specs=[
            pl.BlockSpec(memory_space=pltpu.SMEM), vmem, vmem,
            pl.BlockSpec(memory_space=pl.ANY), pl.BlockSpec(memory_space=pl.ANY),
        ],
        out_specs=vmem,
        scratch_shapes=[
            pltpu.VMEM(piece + (samples,), bf16),
            pltpu.VMEM((lags, chans, 2 * halves * bins, lag_rows), bf16),
            pltpu.VMEM((width_all, width_all), bf16),
            pltpu.VMEM((samples, width_all), bf16),
            pltpu.VMEM(piece + (width_all,), bf16),
            pltpu.VMEM(piece + (width_all,), bf16),
            pltpu.VMEM(piece + (columns,), bf16),
            pltpu.VMEM(piece + (columns,), bf16),
            pltpu.VMEM((times,) + piece + (columns,), bf16),
            pltpu.VMEM((lags,) + piece + (columns,), bf16),
            dma((chans, halves)), dma((lags, chans)),
            dma((chans, halves)), dma((chans, halves)), dma((chans, halves)), dma((chans, halves)),
            dma((times, chans, halves)), dma((times, chans, halves)),
            dma((lags, chans, halves)), dma((lags, chans, halves)),
        ],
        compiler_params=pltpu.CompilerParams(
            collective_id=0, has_side_effects=True, vmem_limit_bytes=58 * 1024 * 1024
        ),
    )(block_map, dead_mask.reshape(1, width_all), records[0, 0], forward_table, inverse_table)
    return stacked.reshape(rounds, width, lag_rows).transpose(2, 0, 1)


def solution(mesh):
    shape = mesh.shape

    def run(records, dead_mask, block_map):
        tables = trig_tables(records.shape[2], shape["chan"], shape["tm"], shape["lag"], HALVES)
        forward_table, inverse_table = (jnp.asarray(a) for a in tables)
        return jax.shard_map(
            body,
            mesh=mesh,
            in_specs=(P(), P(), P(("grp", "tm"), "chan", None, None), P("grp"), P("grp")),
            out_specs=P(("grp", "tm", "lag"), None, "chan"),
            check_vma=False,
        )(forward_table, inverse_table, records, dead_mask, block_map)

    return run
```

```python
import functools
import math

import jax
import jax.numpy as jnp
import ml_dtypes
import numpy as np
from jax import lax
from jax.experimental import pallas as pl
from jax.experimental.pallas import tpu as pltpu
from jax.sharding import PartitionSpec as P

BAND = 16
HALVES = 1
MESH = pl.DeviceIdType.MESH


def trig_tables(samples, chans, times, lags, halves):
    half = samples // 2
    bins = half // (lags * chans * halves)
    rows = np.arange(samples, dtype=np.int64)
    phase = (np.arange(half)[:, None] * rows[None, :]) % samples
    angle = phase.astype(np.float32) * np.float32(2.0 * math.pi / samples)
    cosine = np.cos(angle).astype(ml_dtypes.bfloat16)
    sine = (-np.sin(angle)).astype(ml_dtypes.bfloat16)
    both = np.stack([a.reshape(lags, chans, halves, bins, samples) for a in (cosine, sine)], axis=3)
    forward = both.reshape(lags, chans, halves, 2 * bins, samples)
    inverse = both.reshape(lags, chans, 2 * halves * bins, samples)[..., (rows + half) % samples]
    inverse = inverse.reshape(inverse.shape[:3] + (times * lags, samples // (times * lags)))
    return forward, np.ascontiguousarray(inverse.transpose(3, 0, 1, 2, 4))


def kernel(
    chans, times, lags, rounds, halves, norm,
    map_ref, mask_ref, x_ref, forward_hbm, inverse_hbm, out_ref,
    forward, inverse, pick, ordered, spec_out, spec, cross_out, cross, far, summed,
    forward_sem, inverse_sem, spec_send, spec_recv, cross_send, cross_recv, far_send, far_recv,
    core_send, core_recv,
):
    me, core, group = lax.axis_index("chan"), lax.axis_index("lag"), lax.axis_index("tm")
    samples, width_all = x_ref.shape
    width = width_all // chans
    bins = forward.shape[2] // 2
    columns, lag_rows = out_ref.shape

    def around(index, by, count):
        return lax.rem(index + by + count, count)

    barrier = pltpu.get_barrier_semaphore()
    for axis, index, count in (("chan", me, chans), ("lag", core, lags), ("tm", group, times)):
        for by in range(1, count):
            pl.semaphore_signal(
                barrier, inc=1, device_id={axis: around(index, by, count)}, device_id_type=MESH
            )

    by_reach = sorted(range(1, chans), key=lambda s: abs(s - chans // 2))

    def load_forward(s, h):
        return pltpu.make_async_copy(
            forward_hbm.at[core, around(me, s, chans), h], forward.at[s, h], forward_sem.at[s, h]
        )

    def load_inverse(v, s):
        return pltpu.make_async_copy(
            inverse_hbm.at[group * lags + core, around(core, -v, lags), around(me, -s, chans)],
            inverse.at[v, s], inverse_sem.at[v, s],
        )

    def send_spec(s, h):
        return pltpu.make_async_remote_copy(
            src_ref=spec_out.at[s, h], dst_ref=spec.at[s, h],
            send_sem=spec_send.at[s, h], recv_sem=spec_recv.at[s, h],
            device_id={"chan": around(me, s, chans)}, device_id_type=MESH,
        )

    def send_cross(s, h):
        return pltpu.make_async_remote_copy(
            src_ref=cross_out.at[around(me, s, chans), h], dst_ref=cross.at[s, h],
            send_sem=cross_send.at[s, h], recv_sem=cross_recv.at[s, h],
            device_id={"chan": around(me, s, chans)}, device_id_type=MESH,
        )

    def send_far(u, s, h):
        return pltpu.make_async_remote_copy(
            src_ref=cross.at[s, h], dst_ref=far.at[u, s, h],
            send_sem=far_send.at[u, s, h], recv_sem=far_recv.at[u, s, h],
            device_id={"tm": around(group, u, times)}, device_id_type=MESH,
        )

    def send_core(v, s, h):
        return pltpu.make_async_remote_copy(
            src_ref=summed.at[0, s, h], dst_ref=summed.at[v, s, h],
            send_sem=core_send.at[v, s, h], recv_sem=core_recv.at[v, s, h],
            device_id={"lag": around(core, v, lags)}, device_id_type=MESH,
        )

    def each(low, high, work):
        def step(s, carry):
            work(s)
            return carry

        lax.fori_loop(low, high, step, 0)

    for h in range(halves):
        each(1, chans, lambda s: load_forward(s, h).start())
    for h in range(halves):
        load_forward(0, h).start()
    for v in range(lags):
        each(0, chans, lambda s: load_inverse(v, s).start())

    for p in range(chans):
        source = map_ref[p] * width + lax.broadcasted_iota(jnp.int32, (width, width_all), 0)
        channel = lax.broadcasted_iota(jnp.int32, (width, width_all), 1)
        kept = jnp.where(source == channel, mask_ref[...], 0)
        pick[p * width:(p + 1) * width, :] = kept.astype(jnp.float32).astype(jnp.bfloat16)
    tile = min(512, samples)

    def order(i):
        rows = pl.ds(pl.multiple_of(i * tile, tile), tile)
        ordered[rows, :] = lax.dot_general(
            x_ref[rows, :], pick[...], (((1,), (1,)), ((), ())),
            preferred_element_type=jnp.float32,
        ).astype(jnp.bfloat16)

    each(0, samples // tile, order)

    def transform(s, h):
        load_forward(s, h).wait()
        return jnp.dot(
            forward[s, h], ordered[...], preferred_element_type=jnp.float32
        ).astype(jnp.bfloat16)

    for h in range(halves):
        def transform_out(s):
            spec_out[s, h] = transform(s, h)

        each(1, chans, transform_out)
    pl.semaphore_wait(barrier, chans + lags + times - 3)
    for s in by_reach:
        send_spec(s, 0).start()
    for h in range(halves):
        spec[0, h] = transform(0, h)

    def send_next(s, h):
        send_spec(s, h).wait_send()
        send_spec(s, h + 1).start()

    part = min(32, bins)

    def cross_part(h, i):
        low = pl.multiple_of(i * part, part)
        re_rows = pl.ds(low, part)
        im_rows = pl.ds(pl.multiple_of(bins + i * part, part), part)
        power = jnp.zeros((part, width_all), jnp.float32)
        for f in range(chans):
            re = spec[f, h, re_rows, :].astype(jnp.float32)
            im = spec[f, h, im_rows, :].astype(jnp.float32)
            power = power + (re * re + im * im)
        banded = jnp.sum(power.reshape(part // BAND, BAND, width_all), axis=1, keepdims=True)
        scale = 1.0 / jnp.sqrt(banded / float(chans * BAND) + 1e-06)
        scale = jnp.broadcast_to(scale, (part // BAND, BAND, width_all)).reshape(part, width_all)
        freq_base = ((core * chans + me) * halves + h) * bins + low
        freq = (freq_base + lax.broadcasted_iota(jnp.int32, (part, width_all), 0)).astype(
            jnp.float32
        )
        ramp_width = float(max(samples // 128, 1))
        lower = jnp.clip((freq - float(samples // 256)) / ramp_width, 0.0, 1.0)
        upper = jnp.clip((0.45 * samples - freq) / ramp_width, 0.0, 1.0)
        factor = scale * (lower * upper)
        re_sum = [jnp.zeros((part, width_all), jnp.float32) for _ in range(rounds)]
        im_sum = [jnp.zeros((part, width_all), jnp.float32) for _ in range(rounds)]
        for f in range(chans):
            re = (spec[f, h, re_rows, :].astype(jnp.float32) * factor).astype(jnp.bfloat16)
            im = (spec[f, h, im_rows, :].astype(jnp.float32) * factor).astype(jnp.bfloat16)
            re, im = re.astype(jnp.float32), im.astype(jnp.float32)
            for r in range(rounds):
                re_far = pltpu.roll(re, (r + 1) * width, 1)
                im_far = pltpu.roll(im, (r + 1) * width, 1)
                re_sum[r] = re_sum[r] + (re * re_far + im * im_far)
                im_sum[r] = im_sum[r] + (im * re_far - re * im_far)
        for c in range(chans):
            own = slice(c * width, (c + 1) * width)
            cross_out[c, h, re_rows, :] = jnp.concatenate(
                [a[:, own] for a in re_sum], axis=1
            ).astype(jnp.bfloat16)
            cross_out[c, h, im_rows, :] = jnp.concatenate(
                [a[:, own] for a in im_sum], axis=1
            ).astype(jnp.bfloat16)

    def start_far(s, h):
        for u in range(1, times):
            send_far(u, s, h).start()

    def sum_groups(s, h):
        total = cross[s, h].astype(jnp.float32)
        for u in range(1, times):
            send_far(u, s, h).wait_recv()
            total = total + far[u, s, h].astype(jnp.float32)
        summed[0, s, h] = total.astype(jnp.bfloat16)
        for v in range(1, lags):
            send_core(v, s, h).start()

    def pass_on(s, h):
        send_cross(s, h).wait_recv()
        start_far(s, h)

    for h in range(halves):
        if h + 1 < halves:
            each(1, chans, lambda s: send_next(s, h))
        each(1, chans, lambda s: send_spec(s, h).wait_recv())
        each(0, bins // part, lambda i: cross_part(h, i))
        each(1, chans, lambda s: send_cross(s, h).start())
        cross[0, h] = cross_out[me, h]
        start_far(0, h)
        if h > 0:
            each(0, chans, lambda s: sum_groups(s, h - 1))
        each(1, chans, lambda s: pass_on(s, h))
    each(0, chans, lambda s: sum_groups(s, halves - 1))

    def invert(v):
        each(0, chans, lambda s: load_inverse(v, s).wait())
        depth = chans * halves * 2 * bins
        return lax.dot_general(
            summed[v].reshape(depth, columns), inverse[v].reshape(depth, lag_rows),
            (((0,), (0,)), ((), ())), preferred_element_type=jnp.float32,
        )

    result = invert(0)
    for v in range(1, lags):
        for h in range(halves):
            each(0, chans, lambda s: send_core(v, s, h).wait_recv())
        result = result + invert(v)
    out_ref[...] = result * norm

    for h in range(halves):
        if h + 1 == halves:
            each(1, chans, lambda s: send_spec(s, h).wait_send())
        each(1, chans, lambda s: send_cross(s, h).wait_send())
        for u in range(1, times):
            each(0, chans, lambda s: send_far(u, s, h).wait_send())
        for v in range(1, lags):
            each(0, chans, lambda s: send_core(v, s, h).wait_send())


def body(forward_table, inverse_table, records, dead_mask, block_map):
    chans, lags, times = lax.axis_size("chan"), lax.axis_size("lag"), lax.axis_size("tm")
    samples, width_all = records.shape[2:]
    width = width_all // chans
    rounds = min(4, chans // 2)
    halves = HALVES
    bins = samples // (2 * lags * chans * halves)
    lag_rows = samples // (times * lags)
    columns = rounds * width
    norm = 1.0 / math.sqrt(samples // 2 * chans * times)
    vmem = pl.BlockSpec(memory_space=pltpu.VMEM)
    bf16, dma = jnp.bfloat16, pltpu.SemaphoreType.DMA
    piece = (chans, halves, 2 * bins)
    stacked = pl.pallas_call(
        functools.partial(kernel, chans, times, lags, rounds, halves, norm),
        out_shape=jax.ShapeDtypeStruct((columns, lag_rows), jnp.float32),
        in_specs=[
            pl.BlockSpec(memory_space=pltpu.SMEM), vmem, vmem,
            pl.BlockSpec(memory_space=pl.ANY), pl.BlockSpec(memory_space=pl.ANY),
        ],
        out_specs=vmem,
        scratch_shapes=[
            pltpu.VMEM(piece + (samples,), bf16),
            pltpu.VMEM((lags, chans, 2 * halves * bins, lag_rows), bf16),
            pltpu.VMEM((width_all, width_all), bf16),
            pltpu.VMEM((samples, width_all), bf16),
            pltpu.VMEM(piece + (width_all,), bf16),
            pltpu.VMEM(piece + (width_all,), bf16),
            pltpu.VMEM(piece + (columns,), bf16),
            pltpu.VMEM(piece + (columns,), bf16),
            pltpu.VMEM((times,) + piece + (columns,), bf16),
            pltpu.VMEM((lags,) + piece + (columns,), bf16),
            dma((chans, halves)), dma((lags, chans)),
            dma((chans, halves)), dma((chans, halves)), dma((chans, halves)), dma((chans, halves)),
            dma((times, chans, halves)), dma((times, chans, halves)),
            dma((lags, chans, halves)), dma((lags, chans, halves)),
        ],
        compiler_params=pltpu.CompilerParams(
            collective_id=0, has_side_effects=True, vmem_limit_bytes=58 * 1024 * 1024
        ),
    )(block_map, dead_mask.reshape(1, width_all), records[0, 0], forward_table, inverse_table)
    return stacked.reshape(rounds, width, lag_rows).transpose(2, 0, 1)


def solution(mesh):
    shape = mesh.shape

    def run(records, dead_mask, block_map):
        tables = trig_tables(records.shape[2], shape["chan"], shape["tm"], shape["lag"], HALVES)
        forward_table, inverse_table = (jnp.asarray(a) for a in tables)
        return jax.shard_map(
            body,
            mesh=mesh,
            in_specs=(P(), P(), P(("grp", "tm"), "chan", None, None), P("grp"), P("grp")),
            out_specs=P(("grp", "tm", "lag"), None, "chan"),
            check_vma=False,
        )(forward_table, inverse_table, records, dead_mask, block_map)

    return run
```

```python
import functools
import math

import jax
import jax.numpy as jnp
import ml_dtypes
import numpy as np
from jax import lax
from jax.experimental import pallas as pl
from jax.experimental.pallas import tpu as pltpu
from jax.sharding import PartitionSpec as P

BAND = 16
HALVES = 1
MESH = pl.DeviceIdType.MESH


def trig_tables(samples, chans, times, lags, halves):
    half = samples // 2
    bins = half // (lags * chans * halves)
    rows = np.arange(samples, dtype=np.int64)
    phase = (np.arange(half)[:, None] * rows[None, :]) % samples
    angle = phase.astype(np.float32) * np.float32(2.0 * math.pi / samples)
    cosine = np.cos(angle).astype(ml_dtypes.bfloat16)
    sine = (-np.sin(angle)).astype(ml_dtypes.bfloat16)
    both = np.stack([a.reshape(lags, chans, halves, bins, samples) for a in (cosine, sine)], axis=3)
    forward = both.reshape(lags, chans, halves, 2 * bins, samples)
    inverse = both.reshape(lags, chans, 2 * halves * bins, samples)[..., (rows + half) % samples]
    inverse = inverse.reshape(inverse.shape[:3] + (times * lags, samples // (times * lags)))
    return forward, np.ascontiguousarray(inverse.transpose(3, 0, 1, 2, 4))


def kernel(
    chans, times, lags, rounds, halves, norm,
    map_ref, mask_ref, x_ref, forward_hbm, inverse_hbm, out_ref,
    forward, inverse, pick, ordered, spec_out, spec, cross_out, cross, far, summed,
    forward_sem, inverse_sem, spec_send, spec_recv, cross_send, cross_recv, far_send, far_recv,
    core_send, core_recv,
):
    me, core, group = lax.axis_index("chan"), lax.axis_index("lag"), lax.axis_index("tm")
    samples, width_all = x_ref.shape
    width = width_all // chans
    bins = forward.shape[2] // 2
    columns, lag_rows = out_ref.shape

    def around(index, by, count):
        return lax.rem(index + by + count, count)

    barrier = pltpu.get_barrier_semaphore()
    for axis, index, count in (("chan", me, chans), ("lag", core, lags), ("tm", group, times)):
        for by in range(1, count):
            pl.semaphore_signal(
                barrier, inc=1, device_id={axis: around(index, by, count)}, device_id_type=MESH
            )

    by_reach = sorted(range(1, chans), key=lambda s: abs(s - chans // 2))

    def load_forward(s, h):
        return pltpu.make_async_copy(
            forward_hbm.at[core, around(me, s, chans), h], forward.at[s, h], forward_sem.at[s, h]
        )

    def load_inverse(v, s):
        return pltpu.make_async_copy(
            inverse_hbm.at[group * lags + core, around(core, -v, lags), around(me, -s, chans)],
            inverse.at[v, s], inverse_sem.at[v, s],
        )

    def send_spec(s, h):
        return pltpu.make_async_remote_copy(
            src_ref=spec_out.at[s, h], dst_ref=spec.at[s, h],
            send_sem=spec_send.at[s, h], recv_sem=spec_recv.at[s, h],
            device_id={"chan": around(me, s, chans)}, device_id_type=MESH,
        )

    def send_cross(s, h):
        return pltpu.make_async_remote_copy(
            src_ref=cross_out.at[around(me, s, chans), h], dst_ref=cross.at[s, h],
            send_sem=cross_send.at[s, h], recv_sem=cross_recv.at[s, h],
            device_id={"chan": around(me, s, chans)}, device_id_type=MESH,
        )

    def send_far(u, s, h):
        return pltpu.make_async_remote_copy(
            src_ref=cross.at[s, h], dst_ref=far.at[u, s, h],
            send_sem=far_send.at[u, s, h], recv_sem=far_recv.at[u, s, h],
            device_id={"tm": around(group, u, times)}, device_id_type=MESH,
        )

    def send_core(v, s, h):
        return pltpu.make_async_remote_copy(
            src_ref=summed.at[0, s, h], dst_ref=summed.at[v, s, h],
            send_sem=core_send.at[v, s, h], recv_sem=core_recv.at[v, s, h],
            device_id={"lag": around(core, v, lags)}, device_id_type=MESH,
        )

    def each(low, high, work):
        def step(s, carry):
            work(s)
            return carry

        lax.fori_loop(low, high, step, 0)

    for h in range(halves):
        each(1, chans, lambda s: load_forward(s, h).start())
    for h in range(halves):
        load_forward(0, h).start()
    for v in range(lags):
        each(0, chans, lambda s: load_inverse(v, s).start())

    for p in range(chans):
        source = map_ref[p] * width + lax.broadcasted_iota(jnp.int32, (width, width_all), 0)
        channel = lax.broadcasted_iota(jnp.int32, (width, width_all), 1)
        kept = jnp.where(source == channel, mask_ref[...], 0)
        pick[p * width:(p + 1) * width, :] = kept.astype(jnp.float32).astype(jnp.bfloat16)
    tile = min(512, samples)

    def order(i):
        rows = pl.ds(pl.multiple_of(i * tile, tile), tile)
        ordered[rows, :] = lax.dot_general(
            x_ref[rows, :], pick[...], (((1,), (1,)), ((), ())),
            preferred_element_type=jnp.float32,
        ).astype(jnp.bfloat16)

    each(0, samples // tile, order)

    def transform(s, h):
        load_forward(s, h).wait()
        return jnp.dot(
            forward[s, h], ordered[...], preferred_element_type=jnp.float32
        ).astype(jnp.bfloat16)

    for h in range(halves):
        def transform_out(s):
            spec_out[s, h] = transform(s, h)

        each(1, chans, transform_out)
    pl.semaphore_wait(barrier, chans + lags + times - 3)
    for s in by_reach:
        send_spec(s, 0).start()
    for h in range(halves):
        spec[0, h] = transform(0, h)

    def send_next(s, h):
        send_spec(s, h).wait_send()
        send_spec(s, h + 1).start()

    part = min(32, bins)

    def cross_part(h, i):
        low = pl.multiple_of(i * part, part)
        re_rows = pl.ds(low, part)
        im_rows = pl.ds(pl.multiple_of(bins + i * part, part), part)
        power = jnp.zeros((part, width_all), jnp.float32)
        for f in range(chans):
            re = spec[f, h, re_rows, :].astype(jnp.float32)
            im = spec[f, h, im_rows, :].astype(jnp.float32)
            power = power + (re * re + im * im)
        banded = jnp.sum(power.reshape(part // BAND, BAND, width_all), axis=1, keepdims=True)
        scale = 1.0 / jnp.sqrt(banded / float(chans * BAND) + 1e-06)
        scale = jnp.broadcast_to(scale, (part // BAND, BAND, width_all)).reshape(part, width_all)
        freq_base = ((core * chans + me) * halves + h) * bins + low
        freq = (freq_base + lax.broadcasted_iota(jnp.int32, (part, width_all), 0)).astype(
            jnp.float32
        )
        ramp_width = float(max(samples // 128, 1))
        lower = jnp.clip((freq - float(samples // 256)) / ramp_width, 0.0, 1.0)
        upper = jnp.clip((0.45 * samples - freq) / ramp_width, 0.0, 1.0)
        factor = scale * (lower * upper)
        re_sum = [jnp.zeros((part, width_all), jnp.float32) for _ in range(rounds)]
        im_sum = [jnp.zeros((part, width_all), jnp.float32) for _ in range(rounds)]
        for f in range(chans):
            re = (spec[f, h, re_rows, :].astype(jnp.float32) * factor).astype(jnp.bfloat16)
            im = (spec[f, h, im_rows, :].astype(jnp.float32) * factor).astype(jnp.bfloat16)
            re, im = re.astype(jnp.float32), im.astype(jnp.float32)
            for r in range(rounds):
                re_far = pltpu.roll(re, (r + 1) * width, 1)
                im_far = pltpu.roll(im, (r + 1) * width, 1)
                re_sum[r] = re_sum[r] + (re * re_far + im * im_far)
                im_sum[r] = im_sum[r] + (im * re_far - re * im_far)
        for c in range(chans):
            own = slice(c * width, (c + 1) * width)
            cross_out[c, h, re_rows, :] = jnp.concatenate(
                [a[:, own] for a in re_sum], axis=1
            ).astype(jnp.bfloat16)
            cross_out[c, h, im_rows, :] = jnp.concatenate(
                [a[:, own] for a in im_sum], axis=1
            ).astype(jnp.bfloat16)

    def start_far(s, h):
        for u in range(1, times):
            send_far(u, s, h).start()

    def sum_groups(s, h):
        total = cross[s, h].astype(jnp.float32)
        for u in range(1, times):
            send_far(u, s, h).wait_recv()
            total = total + far[u, s, h].astype(jnp.float32)
        summed[0, s, h] = total.astype(jnp.bfloat16)
        for v in range(1, lags):
            send_core(v, s, h).start()

    def pass_on(s, h):
        send_cross(s, h).wait_recv()
        start_far(s, h)

    for h in range(halves):
        if h + 1 < halves:
            each(1, chans, lambda s: send_next(s, h))
        each(1, chans, lambda s: send_spec(s, h).wait_recv())
        each(0, bins // part, lambda i: cross_part(h, i))
        each(1, chans, lambda s: send_cross(s, h).start())
        cross[0, h] = cross_out[me, h]
        start_far(0, h)
        if h > 0:
            each(0, chans, lambda s: sum_groups(s, h - 1))
        each(1, chans, lambda s: pass_on(s, h))
    each(0, chans, lambda s: sum_groups(s, halves - 1))

    def invert(v):
        each(0, chans, lambda s: load_inverse(v, s).wait())
        depth = chans * halves * 2 * bins
        return lax.dot_general(
            summed[v].reshape(depth, columns), inverse[v].reshape(depth, lag_rows),
            (((0,), (0,)), ((), ())), preferred_element_type=jnp.float32,
        )

    result = invert(0)
    for v in range(1, lags):
        each(0, chans, lambda s: load_inverse(v, s).wait())
        for s in range(chans):
            for h in range(halves):
                send_core(v, s, h).wait_recv()
            result = result + lax.dot_general(
                summed[v, s].reshape(halves * 2 * bins, columns), inverse[v, s],
                (((0,), (0,)), ((), ())), preferred_element_type=jnp.float32,
            )
    out_ref[...] = result * norm

    for h in range(halves):
        if h + 1 == halves:
            each(1, chans, lambda s: send_spec(s, h).wait_send())
        each(1, chans, lambda s: send_cross(s, h).wait_send())
        for u in range(1, times):
            each(0, chans, lambda s: send_far(u, s, h).wait_send())
        for v in range(1, lags):
            each(0, chans, lambda s: send_core(v, s, h).wait_send())


def body(forward_table, inverse_table, records, dead_mask, block_map):
    chans, lags, times = lax.axis_size("chan"), lax.axis_size("lag"), lax.axis_size("tm")
    samples, width_all = records.shape[2:]
    width = width_all // chans
    rounds = min(4, chans // 2)
    halves = HALVES
    bins = samples // (2 * lags * chans * halves)
    lag_rows = samples // (times * lags)
    columns = rounds * width
    norm = 1.0 / math.sqrt(samples // 2 * chans * times)
    vmem = pl.BlockSpec(memory_space=pltpu.VMEM)
    bf16, dma = jnp.bfloat16, pltpu.SemaphoreType.DMA
    piece = (chans, halves, 2 * bins)
    stacked = pl.pallas_call(
        functools.partial(kernel, chans, times, lags, rounds, halves, norm),
        out_shape=jax.ShapeDtypeStruct((columns, lag_rows), jnp.float32),
        in_specs=[
            pl.BlockSpec(memory_space=pltpu.SMEM), vmem, vmem,
            pl.BlockSpec(memory_space=pl.ANY), pl.BlockSpec(memory_space=pl.ANY),
        ],
        out_specs=vmem,
        scratch_shapes=[
            pltpu.VMEM(piece + (samples,), bf16),
            pltpu.VMEM((lags, chans, 2 * halves * bins, lag_rows), bf16),
            pltpu.VMEM((width_all, width_all), bf16),
            pltpu.VMEM((samples, width_all), bf16),
            pltpu.VMEM(piece + (width_all,), bf16),
            pltpu.VMEM(piece + (width_all,), bf16),
            pltpu.VMEM(piece + (columns,), bf16),
            pltpu.VMEM(piece + (columns,), bf16),
            pltpu.VMEM((times,) + piece + (columns,), bf16),
            pltpu.VMEM((lags,) + piece + (columns,), bf16),
            dma((chans, halves)), dma((lags, chans)),
            dma((chans, halves)), dma((chans, halves)), dma((chans, halves)), dma((chans, halves)),
            dma((times, chans, halves)), dma((times, chans, halves)),
            dma((lags, chans, halves)), dma((lags, chans, halves)),
        ],
        compiler_params=pltpu.CompilerParams(
            collective_id=0, has_side_effects=True, vmem_limit_bytes=58 * 1024 * 1024
        ),
    )(block_map, dead_mask.reshape(1, width_all), records[0, 0], forward_table, inverse_table)
    return stacked.reshape(rounds, width, lag_rows).transpose(2, 0, 1)


def solution(mesh):
    shape = mesh.shape

    def run(records, dead_mask, block_map):
        tables = trig_tables(records.shape[2], shape["chan"], shape["tm"], shape["lag"], HALVES)
        forward_table, inverse_table = (jnp.asarray(a) for a in tables)
        return jax.shard_map(
            body,
            mesh=mesh,
            in_specs=(P(), P(), P(("grp", "tm"), "chan", None, None), P("grp"), P("grp")),
            out_specs=P(("grp", "tm", "lag"), None, "chan"),
            check_vma=False,
        )(forward_table, inverse_table, records, dead_mask, block_map)

    return run
```
